32 devices in a mesh: groups: 2 (over y), seq: 4 (over z), tensor: 2 (over x), sub: 2 (over core).
Axes of the slice: x: 2, y: 2, z: 4, core: 2. Of those that a mesh axis runs over, the one named last changes fastest.
Arguments:
- query: bfloat16 [2048, 32, 128], P(('groups', 'seq'), ('tensor', 'sub')), parts along dimension 0, may hold values from -24 to 24
- key_states: bfloat16 [2048, 8, 128], P(('groups', 'seq'), 'tensor'), parts along dimension 0, may hold values from -8.4 to 8.4
- value_states: bfloat16 [2048, 8, 128], P(('groups', 'seq'), 'tensor'), parts along dimension 0, may hold values from -16 to 16
- grad_out: bfloat16 [2048, 32, 128], P(('groups', 'seq'), ('tensor', 'sub')), parts along dimension 0, may hold values from -6 to 6
- block_mask: int32 [16, 17], P(('groups', 'seq')), parts along dimension 0, may hold values from 0 to 1, as said below
Outputs:
- attended: bfloat16 [2048, 32, 128], P(('groups', 'seq'), ('tensor', 'sub')), parts along dimension 0
- query_grad: bfloat16 [2048, 32, 128], P(('groups', 'seq'), ('tensor', 'sub')), parts along dimension 0
- key_grad: bfloat16 [2048, 8, 128], P(('groups', 'seq'), 'tensor'), parts along dimension 0
- value_grad: bfloat16 [2048, 8, 128], P(('groups', 'seq'), 'tensor'), parts along dimension 0
The draws below stay inside these ranges and needn't reach their ends.
There are 2 independent parts, one for each index of `groups`. The reference program is written for one: setup_inputs(seed, part) draws one part's arguments, and reference() takes and returns one part's arrays. A program takes and returns all parts, laid end to end along the dimension named above; each array names one. Nothing has to cross between parts.
Inputs may be any that keep to these rules, and one draw needn't show every extreme that they name: `block_mask`: entries are 0 or 1; entry 0 of every row is 1.
All inputs are finite; a program needn't handle non-finite values.
Results may differ from the reference program's by a relative error of at most 0.012.
The reference program's roundings to bfloat16 on the way (of `weights` and `slope`) count: a program that leaves them out, or rounds other values in their place, can miss the bound.
Values may be sent and summed in bfloat16 or wider, within the bound.
No kernel may reach another device: no remote copies, remote signals or barrier semaphores. Data moves between devices by JAX's collectives and lax.ppermute only.
A program may use at most 64 MiB of HBM per device.

```python
import math
import jax
import jax.numpy as jnp
from jax import lax

HEADS = 32
KV_HEADS = 8
HD = 128
BLOCK = 128
WINDOW = 2048
TOKENS = 1024
NBLK = 8
OFFS = 17


def draw_key_states(key, part):
    key = jax.random.fold_in(key, 1)
    result = jnp.clip(1.4 * jax.random.normal(key, (TOKENS, KV_HEADS, HD), jnp.float32), -8.4, 8.4)
    return result.astype(jnp.bfloat16)


def draw_query(key, part):
    key = jax.random.fold_in(key, 2)
    result = jnp.clip(1.4 * jax.random.normal(key, (TOKENS, HEADS, HD), jnp.float32), -8.4, 8.4)
    return result.astype(jnp.bfloat16)


def draw_block_mask(key, part):
    key = jax.random.fold_in(key, 3)
    drawn_bits = jax.random.randint(key, (NBLK, OFFS), 0, 4)
    column = jnp.arange(OFFS)[None, :]
    return jnp.where((column == 0) | (drawn_bits > 0), 1, 0).astype(jnp.int32)


def shard_levels(key, shape, pieces, smallest, high):
    factor_of = 1.0
    for dim, blocks in pieces:
        heights = jax.random.uniform(jax.random.fold_in(jax.random.fold_in(key, 6), dim), (blocks,), jnp.float32, smallest / len(pieces), high / len(pieces))
        factor_of = factor_of * jnp.repeat(jnp.exp(heights), shape[dim] // blocks).reshape((-1,) + (1,) * (len(shape) - 1 - dim))
    return factor_of


def normal_values(own_key, extent, spread, reach, cuts=(), kind=jnp.bfloat16):
    level = shard_levels(own_key, extent, cuts, -0.22, 0.18) if cuts else 1.0
    array = jax.random.normal(own_key, extent, jnp.float32) * spread * level
    return jnp.minimum(jnp.maximum(array, -reach), reach).astype(kind)


def setup_inputs(seed: int = 0, part: int = 0) -> dict:
    keys = jax.random.split(jax.random.key(seed), 6)
    part_splits = jax.random.split(jax.random.fold_in(keys[5], part), 6)
    return {
        "query": draw_query(jax.random.fold_in(jax.random.fold_in(keys[5], part), 71), part),
        "key_states": draw_key_states(jax.random.fold_in(jax.random.fold_in(keys[5], part), 71), part),
        "value_states": normal_values(part_splits[2], (TOKENS, KV_HEADS, HD), 3.0, 16.0, ((0, 4), (1, 2))),
        "grad_out": normal_values(part_splits[3], (TOKENS, HEADS, HD), 1.0, 6.0, ((0, 4), (1, 4))),
        "block_mask": draw_block_mask(jax.random.fold_in(jax.random.fold_in(keys[5], part), 71), part),
    }


NEGATIVE = -1e+30

def reference(query, key_states, value_states, grad_out, block_mask):
    group_size = HEADS // KV_HEADS
    score_scale = 1.0 / math.sqrt(HD)
    query_span = math.gcd(TOKENS, 512)
    key_span = WINDOW + query_span
    offset_count = WINDOW // BLOCK + 1
    pad_keys = jnp.pad(key_states, ((WINDOW, 0), (0, 0), (0, 0)))
    pad_values = jnp.pad(value_states, ((WINDOW, 0), (0, 0), (0, 0)))

    def one_block(carry, block_number):
        key_accum, value_accum = carry
        row_start = (block_number * query_span).astype(jnp.int32)
        query_rows = lax.dynamic_slice_in_dim(query, row_start, query_span, 0).astype(jnp.float32)
        grad_rows = lax.dynamic_slice_in_dim(grad_out, row_start, query_span, 0).astype(jnp.float32)
        key_rows = jnp.repeat(lax.dynamic_slice_in_dim(pad_keys, row_start, key_span, 0), group_size, axis=1).astype(jnp.float32)
        value_rows = jnp.repeat(lax.dynamic_slice_in_dim(pad_values, row_start, key_span, 0), group_size, axis=1).astype(jnp.float32)
        mask_rows = lax.dynamic_slice_in_dim(block_mask, (row_start // BLOCK).astype(jnp.int32), query_span // BLOCK, 0)
        mask_rows = jnp.repeat(mask_rows, BLOCK, axis=0)
        query_at = row_start + jnp.arange(query_span, dtype=jnp.int32)
        key_at = row_start - WINDOW + jnp.arange(key_span, dtype=jnp.int32)
        token_gap = query_at[:, None] - key_at[None, :]
        lag_blocks = query_at[:, None] // BLOCK - key_at[None, :] // BLOCK
        visible = jnp.take_along_axis(mask_rows, jnp.clip(lag_blocks, 0, offset_count - 1).astype(jnp.int32), axis=1) > 0
        allowed = visible & (token_gap >= 0) & (token_gap < WINDOW) & (key_at[None, :] >= 0)
        scores = jnp.einsum('qhd,khd->hqk', query_rows, key_rows) * score_scale
        masked = jnp.where(allowed[None], scores, NEGATIVE)
        row_max = lax.optimization_barrier(jnp.max(masked, axis=2, keepdims=True))
        row_sum = lax.optimization_barrier(jnp.sum(jnp.exp(masked - row_max), axis=2, keepdims=True))
        log_total = row_max + jnp.log(row_sum)
        exact = jnp.exp(masked - log_total)
        weights = exact.astype(jnp.bfloat16).astype(jnp.float32)
        attended = jnp.einsum('hqk,khd->qhd', weights, value_rows).astype(jnp.bfloat16)
        drift = lax.optimization_barrier(jnp.sum(grad_rows * attended.astype(jnp.float32), axis=2)).T
        pushed = jnp.einsum('qhd,khd->hqk', grad_rows, value_rows)
        slope = (exact * (pushed - drift[:, :, None])).astype(jnp.bfloat16).astype(jnp.float32)
        query_grad = (jnp.einsum('hqk,khd->qhd', slope, key_rows) * score_scale).astype(jnp.bfloat16)
        key_part = jnp.einsum('hqk,qhd->khd', slope, query_rows) * score_scale
        value_part = jnp.einsum('hqk,qhd->khd', weights, grad_rows)
        key_part = lax.optimization_barrier(jnp.sum(key_part.reshape(key_span, KV_HEADS, group_size, HD), axis=2))
        value_part = lax.optimization_barrier(jnp.sum(value_part.reshape(key_span, KV_HEADS, group_size, HD), axis=2))
        key_accum = lax.dynamic_update_slice_in_dim(key_accum, lax.dynamic_slice_in_dim(key_accum, row_start, key_span, 0) + key_part, row_start, 0)
        value_accum = lax.dynamic_update_slice_in_dim(value_accum, lax.dynamic_slice_in_dim(value_accum, row_start, key_span, 0) + value_part, row_start, 0)
        return ((key_accum, value_accum), (attended, query_grad))
    start_accum = jnp.zeros((WINDOW + TOKENS, KV_HEADS, HD), jnp.float32)
    (key_accum, value_accum), (attended, query_grad) = lax.scan(one_block, (start_accum, start_accum), jnp.arange(TOKENS // query_span, dtype=jnp.int32))
    attended = attended.reshape(TOKENS, HEADS, HD)
    query_grad = query_grad.reshape(TOKENS, HEADS, HD)
    key_grad = key_accum[WINDOW:].astype(jnp.bfloat16)
    value_grad = value_accum[WINDOW:].astype(jnp.bfloat16)
    return (attended, query_grad, key_grad, value_grad)
```

```python
import functools
import math

import jax
import jax.numpy as jnp
from jax import lax
from jax.experimental import pallas as pl
from jax.experimental.pallas import tpu as pltpu
from jax.sharding import PartitionSpec as P

HEADS = 32
KV_HEADS = 8
BLOCK = 128
WINDOW = 2048
NEGATIVE = -1e30
LOG2E = 1.4426950408889634

VMEM = pl.BlockSpec(memory_space=pltpu.VMEM)
SMEM = pl.BlockSpec(memory_space=pltpu.SMEM)


def shifted(value, axis, steps):
    count = lax.axis_size(axis)
    first, last = (max(0, -steps), min(count, count - steps))
    return lax.ppermute(value, axis, [(source, source + steps) for source in range(first, last)])


def dot(left, right):
    return jnp.dot(left, right, preferred_element_type=jnp.float32)


def pack_kernel(rows, kv_heads, used, meta, key_in, value_in, *refs):
    outs, wide = (refs[:used], refs[used])
    first = meta[1]
    for place, source in enumerate((key_in, value_in)):
        wide[...] = source[...].astype(jnp.float32)
        for head in range(used):
            picked = wide[pl.ds(first + head, rows, stride=kv_heads), :]
            outs[head][place] = picked.astype(jnp.bfloat16)


def turn_kernel(rows, q_heads, used, query_in, grad_in, *refs):
    outs, wide = (refs[: 4 * used], refs[4 * used])
    per = q_heads // used
    for place, source in enumerate((query_in, grad_in)):
        wide[...] = source[...].astype(jnp.float32)
        for head in range(q_heads):
            picked = wide[pl.ds(head, rows, stride=q_heads), :]
            slot, local = divmod(head, per)
            straight, flipped = outs[4 * slot + 2 * place : 4 * slot + 2 * place + 2]
            straight[pl.ds(local * rows, rows), :] = picked.astype(jnp.bfloat16)
            flipped[:, pl.ds(local * rows, rows)] = picked.T.astype(jnp.bfloat16)


def attend_kernel(rows, per, lags, meta, mask, q_ref, qt_ref, g_ref, gt_ref, *refs):
    pairs = refs[:lags]
    out_ref, qgrad_ref, own_ref = refs[lags : lags + 3]
    terms = refs[lags + 3 : 2 * lags + 2]
    scores, weights, slopes, row_max, row_sum, out_t, qgrad_t = refs[2 * lags + 2 :]
    shard = meta[0]
    blocks = rows // BLOCK
    head_size = q_ref.shape[1]
    scale = 1.0 / math.sqrt(head_size)
    to_exp2 = scale * LOG2E

    def each_lag(step):
        for lag in range(lags):
            if lag == 0:
                step(lag)
            else:
                pl.when(shard >= lag)(functools.partial(step, lag))

    def columns(head):
        return pl.ds(head * rows, rows)

    def fold(op, tile):
        return op(tile.reshape(rows // 8, 8, rows), axis=0)

    row_max[...] = jnp.full(row_max.shape, NEGATIVE, jnp.float32)
    row_sum[...] = jnp.zeros(row_sum.shape, jnp.float32)
    out_t[...] = jnp.zeros(out_t.shape, jnp.float32)
    qgrad_t[...] = jnp.zeros(qgrad_t.shape, jnp.float32)

    def score_step(lag):
        key_pos = lax.broadcasted_iota(jnp.int32, (rows, rows), 0)
        query_pos = lax.broadcasted_iota(jnp.int32, (rows, rows), 1)
        query_block = lax.broadcasted_iota(jnp.int32, (1, rows), 1) // BLOCK
        biases = []
        for key_block in range(blocks):
            bias = jnp.full((1, rows), NEGATIVE, jnp.float32)
            for block in range(blocks):
                distance = lag * blocks + block - key_block
                if 0 <= distance < mask.shape[1]:
                    shown = jnp.where(mask[block, distance] > 0, 0.0, NEGATIVE)
                    bias = jnp.where(query_block == block, shown, bias)
            biases.append(jnp.broadcast_to(bias, (BLOCK, rows)))
        bias = jnp.concatenate(biases, 0)
        gap = query_pos - key_pos + lag * rows
        if lag == 0:
            bias = jnp.where(gap >= 0, bias, NEGATIVE)
        if (lag + 1) * rows > WINDOW:
            bias = jnp.where(gap < WINDOW, bias, NEGATIVE)
        for head in range(per):
            tile = dot(pairs[lag][0], qt_ref[:, columns(head)]) + bias
            scores[lag, :, columns(head)] = tile
            row_max[:, columns(head)] = jnp.maximum(row_max[:, columns(head)], fold(jnp.max, tile))

    each_lag(score_step)
    top = jnp.max(row_max[...], axis=0, keepdims=True) * to_exp2

    def exp_step(lag):
        for head in range(per):
            tile = jnp.exp2(
                scores[lag, :, columns(head)] * to_exp2 - top[:, head * rows : (head + 1) * rows]
            )
            scores[lag, :, columns(head)] = tile
            row_sum[:, columns(head)] += fold(jnp.sum, tile)

    each_lag(exp_step)
    share = 1.0 / jnp.sum(row_sum[...], axis=0, keepdims=True)

    def value_step(lag):
        value_t = pairs[lag][1].T
        for head in range(per):
            tile = scores[lag, :, columns(head)] * share[:, head * rows : (head + 1) * rows]
            scores[lag, :, columns(head)] = tile
            low = tile.astype(jnp.bfloat16)
            weights[:, columns(head)] = low
            out_t[:, columns(head)] += dot(value_t, low)
        part = dot(weights[...], g_ref[...])
        if lag == 0:
            own_ref[1] = part
        else:
            terms[lag - 1][1] = part.astype(jnp.bfloat16)

    each_lag(value_step)
    attended_t = out_t[...].astype(jnp.bfloat16).astype(jnp.float32)
    drift = jnp.sum(attended_t * gt_ref[...].astype(jnp.float32), axis=0, keepdims=True)
    out_ref[...] = attended_t.T.astype(jnp.bfloat16)

    def slope_step(lag):
        key_t = pairs[lag][0].T
        for head in range(per):
            pushed = dot(pairs[lag][1], gt_ref[:, columns(head)])
            tile = scores[lag, :, columns(head)] * (
                pushed - drift[:, head * rows : (head + 1) * rows]
            )
            low = tile.astype(jnp.bfloat16)
            slopes[:, columns(head)] = low
            qgrad_t[:, columns(head)] += dot(key_t, low)
        part = dot(slopes[...], q_ref[...]) * scale
        if lag == 0:
            own_ref[0] = part
        else:
            terms[lag - 1][0] = part.astype(jnp.bfloat16)

    each_lag(slope_step)
    qgrad_ref[...] = (qgrad_t[...] * scale).T.astype(jnp.bfloat16)


def unturn_kernel(rows, q_heads, used, *refs):
    sources, outs, wide = (refs[: 2 * used], refs[2 * used : 2 * used + 2], refs[-1])
    per = q_heads // used
    for place, target in enumerate(outs):
        for head in range(q_heads):
            slot, local = divmod(head, per)
            tile = sources[2 * slot + place][pl.ds(local * rows, rows), :]
            wide[pl.ds(head, rows, stride=q_heads), :] = tile.astype(jnp.float32)
        target[...] = wide[...].astype(jnp.bfloat16)


def join_kernel(rows, kv_heads, used, meta, *refs):
    own, other = (refs[:used], refs[used : 2 * used])
    outs, wide = (refs[2 * used : 2 * used + 2], refs[-1])
    first = meta[1]
    for place, target in enumerate(outs):
        for head in range(used):
            mine = own[head][place].astype(jnp.float32)
            theirs = other[head][place].astype(jnp.float32)
            if used == kv_heads:
                wide[pl.ds(head, rows, stride=kv_heads), :] = mine + theirs
            else:
                away = kv_heads - used - first
                wide[pl.ds(first + head, rows, stride=kv_heads), :] = mine
                wide[pl.ds(away + head, rows, stride=kv_heads), :] = theirs
        target[...] = wide[...].astype(jnp.bfloat16)


def body(query, key_states, value_states, grad_out, block_mask):
    rows, q_heads, head_size = query.shape
    kv_heads = key_states.shape[1]
    lags = min(WINDOW // rows, lax.axis_size("seq") - 1) + 1
    used = max(1, q_heads * KV_HEADS // HEADS)
    per = q_heads // used
    width = per * rows
    low, wide = (jnp.bfloat16, jnp.float32)
    core_first = lax.axis_index("sub") * q_heads * KV_HEADS // HEADS
    meta = jnp.stack([lax.axis_index("seq"), core_first]).astype(jnp.int32)
    params = pltpu.CompilerParams(vmem_limit_bytes=28 * 2**20)

    def call(kernel, ins, outs, scratch, flops=0, moved=2**20):
        return pl.pallas_call(
            kernel,
            in_specs=ins,
            out_specs=[VMEM] * len(outs),
            out_shape=[jax.ShapeDtypeStruct(*o) for o in outs],
            scratch_shapes=[pltpu.VMEM(*s) for s in scratch],
            compiler_params=params,
            cost_estimate=pl.CostEstimate(flops=flops, bytes_accessed=moved, transcendentals=0),
        )

    packed = call(
        functools.partial(pack_kernel, rows, kv_heads, used),
        [SMEM, VMEM, VMEM],
        [((2, rows, head_size), low)] * used,
        [((rows * kv_heads, head_size), wide)],
    )(meta, key_states.reshape(-1, head_size), value_states.reshape(-1, head_size))
    pairs = [[pair] + [shifted(pair, "seq", lag) for lag in range(1, lags)] for pair in packed]

    turned = call(
        functools.partial(turn_kernel, rows, q_heads, used),
        [VMEM, VMEM],
        [((width, head_size), low), ((head_size, width), low)] * (2 * used),
        [((rows * q_heads, head_size), wide)],
    )(query.reshape(-1, head_size), grad_out.reshape(-1, head_size))

    results, sums = ([], [])
    for head in range(used):
        attended, qgrad, own, *terms = call(
            functools.partial(attend_kernel, rows, per, lags),
            [SMEM, SMEM] + [VMEM] * (4 + lags),
            [((width, head_size), low)] * 2
            + [((2, rows, head_size), wide)]
            + [((2, rows, head_size), low)] * (lags - 1),
            [
                ((lags, rows, width), wide),
                ((rows, width), low),
                ((rows, width), low),
                ((8, width), wide),
                ((8, width), wide),
                ((head_size, width), wide),
                ((head_size, width), wide),
            ],
            flops=12 * lags * rows * width * head_size,
        )(meta, block_mask, *turned[4 * head : 4 * head + 4], *pairs[head])
        results += [attended, qgrad]
        for lag in range(lags - 1, 0, -1):
            own = own + shifted(terms[lag - 1], "seq", -lag).astype(wide)
        sums.append(own.astype(low))

    attended, qgrad = call(
        functools.partial(unturn_kernel, rows, q_heads, used),
        [VMEM] * (2 * used),
        [((rows * q_heads, head_size), low)] * 2,
        [((rows * q_heads, head_size), wide)],
    )(*results)
    others = [lax.ppermute(value, "sub", [(0, 1), (1, 0)]) for value in sums]
    key_grad, value_grad = call(
        functools.partial(join_kernel, rows, kv_heads, used),
        [SMEM] + [VMEM] * (2 * used),
        [((rows * kv_heads, head_size), low)] * 2,
        [((rows * kv_heads, head_size), wide)],
    )(meta, *sums, *others)
    return (
        attended.reshape(rows, q_heads, head_size),
        qgrad.reshape(rows, q_heads, head_size),
        key_grad.reshape(rows, kv_heads, head_size),
        value_grad.reshape(rows, kv_heads, head_size),
    )


def solution(mesh):
    q_spec = P(("groups", "seq"), ("tensor", "sub"), None)
    kv_spec = P(("groups", "seq"), "tensor", None)
    return jax.shard_map(
        body,
        mesh=mesh,
        in_specs=(q_spec, kv_spec, kv_spec, q_spec, P(("groups", "seq"), None)),
        out_specs=(q_spec, q_spec, kv_spec, kv_spec),
        check_vma=False,
    )
```

```python
import functools
import math

import jax
import jax.numpy as jnp
from jax import lax
from jax.experimental import pallas as pl
from jax.experimental.pallas import tpu as pltpu
from jax.sharding import PartitionSpec as P

HEADS = 32
KV_HEADS = 8
BLOCK = 128
WINDOW = 2048
NEGATIVE = -1e30
LOG2E = 1.4426950408889634

VMEM = pl.BlockSpec(memory_space=pltpu.VMEM)
SMEM = pl.BlockSpec(memory_space=pltpu.SMEM)
HBM = pl.BlockSpec(memory_space=pltpu.HBM)


def shifted(value, axis, steps):
    count = lax.axis_size(axis)
    first, last = (max(0, -steps), min(count, count - steps))
    return lax.ppermute(value, axis, [(source, source + steps) for source in range(first, last)])


def after(value, *others):
    return lax.optimization_barrier((value, *others))[0]


def dot(left, right):
    return jnp.dot(left, right, preferred_element_type=jnp.float32)


def pack_kernel(rows, kv_heads, used, meta, key_in, value_in, *refs):
    outs, (low, wide, sems) = (refs[:used], refs[used:])
    copies = [
        pltpu.make_async_copy(source, low.at[place], sems.at[place])
        for place, source in enumerate((key_in, value_in))
    ]
    for copy in copies:
        copy.start()
    for place, copy in enumerate(copies):
        copy.wait()
        wide[...] = low[place].astype(jnp.float32)
        for head in range(used):
            picked = wide[pl.ds(meta[1] + head, rows, stride=kv_heads), :]
            outs[head][place] = picked.astype(jnp.bfloat16)


def turn_kernel(rows, q_heads, used, query_in, grad_in, *refs):
    outs, wide = (refs[: 4 * used], refs[4 * used])
    per = q_heads // used
    for place, source in enumerate((query_in, grad_in)):
        wide[...] = source[...].astype(jnp.float32)
        for head in range(q_heads):
            picked = wide[pl.ds(head, rows, stride=q_heads), :]
            slot, local = divmod(head, per)
            straight, flipped = outs[4 * slot + 2 * place : 4 * slot + 2 * place + 2]
            straight[pl.ds(local * rows, rows), :] = picked.astype(jnp.bfloat16)
            flipped[:, pl.ds(local * rows, rows)] = picked.T.astype(jnp.bfloat16)


def attend_part(count, rows, per, lags, offsets, meta, q_ref, qt_ref, g_ref, gt_ref, *refs):
    pairs = refs[:lags]
    out_ref, qgrad_ref, own_ref = refs[lags : lags + 3]
    terms = refs[lags + 3 : 2 * lags + 2]
    powers, low_tile, tops, sums, out_t, qgrad_t = refs[2 * lags + 2 :]
    shard = meta[0]
    blocks = rows // BLOCK
    head_size = q_ref.shape[1]
    scale = 1.0 / math.sqrt(head_size)
    to_exp2 = scale * LOG2E

    def each_lag(step):
        if count is None:
            step(0)
            for lag in range(1, lags):
                pl.when(shard >= lag)(functools.partial(step, lag))
        else:
            for lag in range(count):
                step(lag)

    def columns(head):
        return slice(head * rows, (head + 1) * rows)

    def fold(op, tile):
        return op(op(tile.reshape(-1, 8, tile.shape[1]), axis=0), axis=0, keepdims=True)

    tops[...] = jnp.full(tops.shape, NEGATIVE, jnp.float32)
    sums[...] = jnp.zeros(sums.shape, jnp.float32)
    out_t[...] = jnp.zeros(out_t.shape, jnp.float32)
    qgrad_t[...] = jnp.zeros(qgrad_t.shape, jnp.float32)

    def score_step(lag):
        query_pos = lax.broadcasted_iota(jnp.int32, (BLOCK, rows), 1)
        key_pos = lax.broadcasted_iota(jnp.int32, (BLOCK, rows), 0)
        query_block = lax.broadcasted_iota(jnp.int32, (1, rows), 1) // BLOCK
        for head in range(per):
            both = dot(pairs[lag][0], qt_ref[:, columns(head)])
            for block in range(blocks):
                tile = both[block * BLOCK : (block + 1) * BLOCK]
                gap = query_pos - key_pos + (lag * rows - block * BLOCK)
                if lag == 0:
                    tile = jnp.where(gap >= 0, tile, NEGATIVE)
                if (lag + 1) * rows > WINDOW:
                    tile = jnp.where(gap < WINDOW, tile, NEGATIVE)
                top = fold(jnp.max, tile)
                power = jnp.exp2((tile - top) * to_exp2)
                powers[lag, block * BLOCK : (block + 1) * BLOCK, columns(head)] = power
                shown = jnp.zeros((1, rows), jnp.int32)
                for seen in range(blocks):
                    distance = lag * blocks + seen - block
                    if 0 <= distance < offsets:
                        shown = jnp.where(query_block == seen, meta[2 + seen * offsets + distance], shown)
                place = lag * blocks + block
                tops[place : place + 1, columns(head)] = jnp.where(shown > 0, top, NEGATIVE)
                sums[place : place + 1, columns(head)] = fold(jnp.sum, power)

    each_lag(score_step)
    top = jnp.max(tops[...], axis=0, keepdims=True)
    factor = jnp.exp2((tops[...] - top) * to_exp2)
    tops[...] = factor / jnp.sum(factor * sums[...], axis=0, keepdims=True)

    def weigh(lag, head):
        tiles = []
        for block in range(blocks):
            place = lag * blocks + block
            power = powers[lag, block * BLOCK : (block + 1) * BLOCK, columns(head)]
            tiles.append(power * tops[place : place + 1, columns(head)])
        return jnp.concatenate(tiles, 0)

    def value_step(lag):
        value_t = pairs[lag][1].T
        for head in range(per):
            low = weigh(lag, head).astype(jnp.bfloat16)
            low_tile[lag, :, columns(head)] = low
            out_t[:, columns(head)] += dot(value_t, low)
        part = dot(low_tile[lag], g_ref[...])
        if lag == 0:
            own_ref[1] = part
        else:
            terms[lag - 1][1] = part.astype(jnp.bfloat16)

    each_lag(value_step)
    attended_t = out_t[...].astype(jnp.bfloat16).astype(jnp.float32)
    drift = jnp.sum(attended_t * gt_ref[...].astype(jnp.float32), axis=0, keepdims=True)
    out_ref[...] = attended_t.T.astype(jnp.bfloat16)

    def push_step(lag):
        for head in range(per):
            pushed = dot(pairs[lag][1], gt_ref[:, columns(head)])
            low = (weigh(lag, head) * (pushed - drift[:, columns(head)])).astype(jnp.bfloat16)
            low_tile[lag, :, columns(head)] = low

    each_lag(push_step)

    def slope_step(lag):
        key_t = pairs[lag][0].T
        qgrad_t[...] += dot(key_t, low_tile[lag])
        part = dot(low_tile[lag], q_ref[...]) * scale
        if lag == 0:
            own_ref[0] = part
        else:
            terms[lag - 1][0] = part.astype(jnp.bfloat16)

    each_lag(slope_step)
    qgrad_ref[...] = (qgrad_t[...] * scale).T.astype(jnp.bfloat16)


def attend_kernel(rows, per, lags, offsets, meta, *refs):
    if lags > 4:
        attend_part(None, rows, per, lags, offsets, meta, *refs)
        return
    there = jnp.minimum(meta[0] + 1, lags)
    for count in range(1, lags + 1):
        part = functools.partial(attend_part, count, rows, per, lags, offsets)
        pl.when(there == count)(functools.partial(part, meta, *refs))


def unturn_kernel(rows, q_heads, used, *refs):
    sources, outs, wide = (refs[: 2 * used], refs[2 * used : 2 * used + 2], refs[-1])
    per = q_heads // used
    for place, target in enumerate(outs):
        for head in range(q_heads):
            slot, local = divmod(head, per)
            tile = sources[2 * slot + place][pl.ds(local * rows, rows), :]
            wide[pl.ds(head, rows, stride=q_heads), :] = tile.astype(jnp.float32)
        target[...] = wide[...].astype(jnp.bfloat16)


def join_kernel(rows, kv_heads, used, meta, *refs):
    own, other = (refs[:used], refs[used : 2 * used])
    outs, wide = (refs[2 * used : 2 * used + 2], refs[-1])
    first = meta[1]
    for place, target in enumerate(outs):
        for head in range(used):
            mine = own[head][place].astype(jnp.float32)
            theirs = other[head][place].astype(jnp.float32)
            if used == kv_heads:
                wide[pl.ds(head, rows, stride=kv_heads), :] = mine + theirs
            else:
                away = kv_heads - used - first
                wide[pl.ds(first + head, rows, stride=kv_heads), :] = mine
                wide[pl.ds(away + head, rows, stride=kv_heads), :] = theirs
        target[...] = wide[...].astype(jnp.bfloat16)


def body(query, key_states, value_states, grad_out, block_mask):
    rows, q_heads, head_size = query.shape
    kv_heads = key_states.shape[1]
    lags = min(WINDOW // rows, lax.axis_size("seq") - 1) + 1
    used = max(1, q_heads * KV_HEADS // HEADS)
    per = q_heads // used
    width = per * rows
    low, wide = (jnp.bfloat16, jnp.float32)
    core_first = lax.axis_index("sub") * q_heads * KV_HEADS // HEADS
    shard = lax.axis_index("seq")
    meta = jnp.stack([shard, core_first]).astype(jnp.int32)

    def call(kernel, ins, outs, scratch, flops=0, moved=2**20, limit=28):
        return pl.pallas_call(
            kernel,
            in_specs=ins,
            out_specs=[VMEM] * len(outs),
            out_shape=[jax.ShapeDtypeStruct(*o) for o in outs],
            scratch_shapes=[pltpu.VMEM(*s) if isinstance(s, tuple) else s for s in scratch],
            compiler_params=pltpu.CompilerParams(vmem_limit_bytes=limit * 2**20),
            cost_estimate=pl.CostEstimate(flops=flops, bytes_accessed=moved, transcendentals=0),
        )

    packed = call(
        functools.partial(pack_kernel, rows, kv_heads, used),
        [SMEM, HBM, HBM],
        [((2, rows, head_size), low)] * used,
        [
            ((2, rows * kv_heads, head_size), low),
            ((rows * kv_heads, head_size), wide),
            pltpu.SemaphoreType.DMA((2,)),
        ],
        limit=28,
    )(meta, key_states.reshape(-1, head_size), value_states.reshape(-1, head_size))
    turned = call(
        functools.partial(turn_kernel, rows, q_heads, used),
        [VMEM, VMEM],
        [((width, head_size), low), ((head_size, width), low)] * (2 * used),
        [((rows * q_heads, head_size), wide)],
    )(query.reshape(-1, head_size), grad_out.reshape(-1, head_size))
    full_meta = jnp.concatenate([meta, after(block_mask, *packed).reshape(-1)])

    results, sums = ([], [])
    for head in range(used):
        pairs = [packed[head]] + [shifted(packed[head], "seq", lag) for lag in range(1, lags)]
        attended, qgrad, own, *terms = call(
            functools.partial(attend_kernel, rows, per, lags, block_mask.shape[1]),
            [SMEM] + [VMEM] * (4 + lags),
            [((width, head_size), low)] * 2
            + [((2, rows, head_size), wide)]
            + [((2, rows, head_size), low)] * (lags - 1),
            [
                ((lags, rows, width), wide),
                ((lags, rows, width), low),
                ((lags * (rows // BLOCK), width), wide),
                ((lags * (rows // BLOCK), width), wide),
                ((head_size, width), wide),
                ((head_size, width), wide),
            ],
            flops=12 * lags * rows * width * head_size,
        )(full_meta, *turned[4 * head : 4 * head + 4], *pairs)
        results += [attended, qgrad]
        for lag in range(lags - 1, 0, -1):
            own = own + shifted(terms[lag - 1], "seq", -lag).astype(wide)
        sums.append(own.astype(low))

    attended, qgrad = call(
        functools.partial(unturn_kernel, rows, q_heads, used),
        [VMEM] * (2 * used),
        [((rows * q_heads, head_size), low)] * 2,
        [((rows * q_heads, head_size), wide)],
    )(*results)
    others = [lax.ppermute(value, "sub", [(0, 1), (1, 0)]) for value in sums]
    key_grad, value_grad = call(
        functools.partial(join_kernel, rows, kv_heads, used),
        [SMEM] + [VMEM] * (2 * used),
        [((rows * kv_heads, head_size), low)] * 2,
        [((rows * kv_heads, head_size), wide)],
    )(meta, *sums, *others)
    return (
        attended.reshape(rows, q_heads, head_size),
        qgrad.reshape(rows, q_heads, head_size),
        key_grad.reshape(rows, kv_heads, head_size),
        value_grad.reshape(rows, kv_heads, head_size),
    )


def solution(mesh):
    q_spec = P(("groups", "seq"), ("tensor", "sub"), None)
    kv_spec = P(("groups", "seq"), "tensor", None)
    return jax.shard_map(
        body,
        mesh=mesh,
        in_specs=(q_spec, kv_spec, kv_spec, q_spec, P(("groups", "seq"), None)),
        out_specs=(q_spec, q_spec, kv_spec, kv_spec),
        check_vma=False,
    )
```

```python
import functools
import math

import jax
import jax.numpy as jnp
from jax import lax
from jax.experimental import pallas as pl
from jax.experimental.pallas import tpu as pltpu
from jax.sharding import PartitionSpec as P

HEADS = 32
KV_HEADS = 8
BLOCK = 128
WINDOW = 2048
NEGATIVE = -1e30
LOG2E = 1.4426950408889634

VMEM = pl.BlockSpec(memory_space=pltpu.VMEM)
SMEM = pl.BlockSpec(memory_space=pltpu.SMEM)


def shifted(value, axis, steps):
    count = lax.axis_size(axis)
    first, last = (max(0, -steps), min(count, count - steps))
    return lax.ppermute(value, axis, [(source, source + steps) for source in range(first, last)])


def after(value, *others):
    return lax.optimization_barrier((value, *others))[0]


def dot(left, right):
    return jnp.dot(left, right, preferred_element_type=jnp.float32)


def turn_kernel(rows, q_heads, used, query_in, grad_in, *refs):
    outs, wide = (refs[: 4 * used], refs[4 * used])
    per = q_heads // used
    for place, source in enumerate((query_in, grad_in)):
        wide[...] = source[...].astype(jnp.float32)
        for head in range(q_heads):
            picked = wide[pl.ds(head, rows, stride=q_heads), :]
            slot, local = divmod(head, per)
            straight, flipped = outs[4 * slot + 2 * place : 4 * slot + 2 * place + 2]
            straight[pl.ds(local * rows, rows), :] = picked.astype(jnp.bfloat16)
            flipped[:, pl.ds(local * rows, rows)] = picked.T.astype(jnp.bfloat16)


def attend_part(count, rows, per, lags, offsets, meta, q_ref, qt_ref, g_ref, gt_ref, *refs):
    pairs = refs[:lags]
    out_ref, qgrad_ref, own_ref = refs[lags : lags + 3]
    terms = refs[lags + 3 : 2 * lags + 2]
    powers, low_tile, tops, sums, out_t, qgrad_t = refs[2 * lags + 2 :]
    shard = meta[0]
    blocks = rows // BLOCK
    head_size = q_ref.shape[1]
    scale = 1.0 / math.sqrt(head_size)
    to_exp2 = scale * LOG2E

    def each_lag(step):
        if count is None:
            step(0)
            for lag in range(1, lags):
                pl.when(shard >= lag)(functools.partial(step, lag))
        else:
            for lag in range(count):
                step(lag)

    def columns(head):
        return slice(head * rows, (head + 1) * rows)

    def fold(op, tile):
        return op(op(tile.reshape(-1, 8, tile.shape[1]), axis=0), axis=0, keepdims=True)

    tops[...] = jnp.full(tops.shape, NEGATIVE, jnp.float32)
    sums[...] = jnp.zeros(sums.shape, jnp.float32)
    out_t[...] = jnp.zeros(out_t.shape, jnp.float32)
    qgrad_t[...] = jnp.zeros(qgrad_t.shape, jnp.float32)

    def score_step(lag):
        query_pos = lax.broadcasted_iota(jnp.int32, (BLOCK, rows), 1)
        key_pos = lax.broadcasted_iota(jnp.int32, (BLOCK, rows), 0)
        query_block = lax.broadcasted_iota(jnp.int32, (1, rows), 1) // BLOCK
        for head in range(per):
            both = dot(pairs[lag][0], qt_ref[:, columns(head)])
            for block in range(blocks):
                tile = both[block * BLOCK : (block + 1) * BLOCK]
                gap = query_pos - key_pos + (lag * rows - block * BLOCK)
                if lag == 0:
                    tile = jnp.where(gap >= 0, tile, NEGATIVE)
                if (lag + 1) * rows > WINDOW:
                    tile = jnp.where(gap < WINDOW, tile, NEGATIVE)
                top = fold(jnp.max, tile)
                power = jnp.exp2((tile - top) * to_exp2)
                powers[lag, block * BLOCK : (block + 1) * BLOCK, columns(head)] = power
                shown = jnp.zeros((1, rows), jnp.int32)
                for seen in range(blocks):
                    distance = lag * blocks + seen - block
                    if 0 <= distance < offsets:
                        shown = jnp.where(query_block == seen, meta[2 + seen * offsets + distance], shown)
                place = lag * blocks + block
                tops[place : place + 1, columns(head)] = jnp.where(shown > 0, top, NEGATIVE)
                sums[place : place + 1, columns(head)] = fold(jnp.sum, power)

    each_lag(score_step)
    top = jnp.max(tops[...], axis=0, keepdims=True)
    factor = jnp.exp2((tops[...] - top) * to_exp2)
    tops[...] = factor / jnp.sum(factor * sums[...], axis=0, keepdims=True)

    def weigh(lag, head):
        tiles = []
        for block in range(blocks):
            place = lag * blocks + block
            power = powers[lag, block * BLOCK : (block + 1) * BLOCK, columns(head)]
            tiles.append(power * tops[place : place + 1, columns(head)])
        return jnp.concatenate(tiles, 0)

    def value_step(lag):
        value_t = pairs[lag][1].T
        for head in range(per):
            low = weigh(lag, head).astype(jnp.bfloat16)
            low_tile[lag, :, columns(head)] = low
            out_t[:, columns(head)] += dot(value_t, low)
        part = dot(low_tile[lag], g_ref[...])
        if lag == 0:
            own_ref[1] = part
        else:
            terms[lag - 1][1] = part.astype(jnp.bfloat16)

    each_lag(value_step)
    attended_t = out_t[...].astype(jnp.bfloat16).astype(jnp.float32)
    drift = jnp.sum(attended_t * gt_ref[...].astype(jnp.float32), axis=0, keepdims=True)
    out_ref[...] = attended_t.T.astype(jnp.bfloat16)

    def push_step(lag):
        for head in range(per):
            pushed = dot(pairs[lag][1], gt_ref[:, columns(head)])
            low = (weigh(lag, head) * (pushed - drift[:, columns(head)])).astype(jnp.bfloat16)
            low_tile[lag, :, columns(head)] = low

    each_lag(push_step)

    def slope_step(lag):
        key_t = pairs[lag][0].T
        qgrad_t[...] += dot(key_t, low_tile[lag])
        part = dot(low_tile[lag], q_ref[...]) * scale
        if lag == 0:
            own_ref[0] = part
        else:
            terms[lag - 1][0] = part.astype(jnp.bfloat16)

    each_lag(slope_step)
    qgrad_ref[...] = (qgrad_t[...] * scale).T.astype(jnp.bfloat16)


def attend_kernel(rows, per, lags, offsets, meta, *refs):
    if lags > 4:
        attend_part(None, rows, per, lags, offsets, meta, *refs)
        return
    there = jnp.minimum(meta[0] + 1, lags)
    for count in range(1, lags + 1):
        part = functools.partial(attend_part, count, rows, per, lags, offsets)
        pl.when(there == count)(functools.partial(part, meta, *refs))


def unturn_kernel(rows, q_heads, used, *refs):
    sources, outs, wide = (refs[: 2 * used], refs[2 * used : 2 * used + 2], refs[-1])
    per = q_heads // used
    for place, target in enumerate(outs):
        for head in range(q_heads):
            slot, local = divmod(head, per)
            tile = sources[2 * slot + place][pl.ds(local * rows, rows), :]
            wide[pl.ds(head, rows, stride=q_heads), :] = tile.astype(jnp.float32)
        target[...] = wide[...].astype(jnp.bfloat16)


def join_kernel(rows, kv_heads, used, meta, *refs):
    own, other = (refs[:used], refs[used : 2 * used])
    outs, wide = (refs[2 * used : 2 * used + 2], refs[-1])
    first = meta[1]
    for place, target in enumerate(outs):
        for head in range(used):
            mine = own[head][place].astype(jnp.float32)
            theirs = other[head][place].astype(jnp.float32)
            if used == kv_heads:
                wide[pl.ds(head, rows, stride=kv_heads), :] = mine + theirs
            else:
                away = kv_heads - used - first
                wide[pl.ds(first + head, rows, stride=kv_heads), :] = mine
                wide[pl.ds(away + head, rows, stride=kv_heads), :] = theirs
        target[...] = wide[...].astype(jnp.bfloat16)


def body(query, key_states, value_states, grad_out, block_mask):
    rows, q_heads, head_size = query.shape
    kv_heads = key_states.shape[1]
    lags = min(WINDOW // rows, lax.axis_size("seq") - 1) + 1
    used = max(1, q_heads * KV_HEADS // HEADS)
    per = q_heads // used
    width = per * rows
    low, wide = (jnp.bfloat16, jnp.float32)
    core_first = lax.axis_index("sub") * q_heads * KV_HEADS // HEADS
    shard = lax.axis_index("seq")
    meta = jnp.stack([shard, core_first]).astype(jnp.int32)

    def call(kernel, ins, outs, scratch, flops=0, moved=2**20, limit=28):
        return pl.pallas_call(
            kernel,
            in_specs=ins,
            out_specs=[VMEM] * len(outs),
            out_shape=[jax.ShapeDtypeStruct(*o) for o in outs],
            scratch_shapes=[pltpu.VMEM(*s) if isinstance(s, tuple) else s for s in scratch],
            compiler_params=pltpu.CompilerParams(vmem_limit_bytes=limit * 2**20),
            cost_estimate=pl.CostEstimate(flops=flops, bytes_accessed=moved, transcendentals=0),
        )

    packed = []
    for head in range(used - 1, -1, -1):
        states = [after(states, *packed[:1]) for states in (key_states, value_states)]
        picked = [lax.dynamic_index_in_dim(heads, core_first + head, 1, keepdims=False) for heads in states]
        packed.insert(0, jnp.stack(picked, 0))
    turned = call(
        functools.partial(turn_kernel, rows, q_heads, used),
        [VMEM, VMEM],
        [((width, head_size), low), ((head_size, width), low)] * (2 * used),
        [((rows * q_heads, head_size), wide)],
    )(query.reshape(-1, head_size), grad_out.reshape(-1, head_size))
    full_meta = jnp.concatenate([meta, after(block_mask, *packed).reshape(-1)])

    results, sums = ([], [])
    for head in range(used):
        pairs = [packed[head]] + [shifted(packed[head], "seq", lag) for lag in range(1, lags)]
        attended, qgrad, own, *terms = call(
            functools.partial(attend_kernel, rows, per, lags, block_mask.shape[1]),
            [SMEM] + [VMEM] * (4 + lags),
            [((width, head_size), low)] * 2
            + [((2, rows, head_size), wide)]
            + [((2, rows, head_size), low)] * (lags - 1),
            [
                ((lags, rows, width), wide),
                ((lags, rows, width), low),
                ((lags * (rows // BLOCK), width), wide),
                ((lags * (rows // BLOCK), width), wide),
                ((head_size, width), wide),
                ((head_size, width), wide),
            ],
            flops=12 * lags * rows * width * head_size,
        )(full_meta, *turned[4 * head : 4 * head + 4], *pairs)
        results += [attended, qgrad]
        for lag in range(lags - 1, 0, -1):
            own = own + shifted(terms[lag - 1], "seq", -lag).astype(wide)
        sums.append(own.astype(low))

    attended, qgrad = call(
        functools.partial(unturn_kernel, rows, q_heads, used),
        [VMEM] * (2 * used),
        [((rows * q_heads, head_size), low)] * 2,
        [((rows * q_heads, head_size), wide)],
    )(*results)
    others = [lax.ppermute(value, "sub", [(0, 1), (1, 0)]) for value in sums]
    key_grad, value_grad = call(
        functools.partial(join_kernel, rows, kv_heads, used),
        [SMEM] + [VMEM] * (2 * used),
        [((rows * kv_heads, head_size), low)] * 2,
        [((rows * kv_heads, head_size), wide)],
    )(meta, *sums, *others)
    return (
        attended.reshape(rows, q_heads, head_size),
        qgrad.reshape(rows, q_heads, head_size),
        key_grad.reshape(rows, kv_heads, head_size),
        value_grad.reshape(rows, kv_heads, head_size),
    )


def solution(mesh):
    q_spec = P(("groups", "seq"), ("tensor", "sub"), None)
    kv_spec = P(("groups", "seq"), "tensor", None)
    return jax.shard_map(
        body,
        mesh=mesh,
        in_specs=(q_spec, kv_spec, kv_spec, q_spec, P(("groups", "seq"), None)),
        out_specs=(q_spec, q_spec, kv_spec, kv_spec),
        check_vma=False,
    )
```

```python
import functools
import math

import jax
import jax.numpy as jnp
from jax import lax
from jax.experimental import pallas as pl
from jax.experimental.pallas import tpu as pltpu
from jax.sharding import PartitionSpec as P

HEADS = 32
KV_HEADS = 8
BLOCK = 128
WINDOW = 2048
NEGATIVE = -1e30
LOG2E = 1.4426950408889634

VMEM = pl.BlockSpec(memory_space=pltpu.VMEM)
SMEM = pl.BlockSpec(memory_space=pltpu.SMEM)


def shifted(value, axis, steps):
    count = lax.axis_size(axis)
    first, last = (max(0, -steps), min(count, count - steps))
    return lax.ppermute(value, axis, [(source, source + steps) for source in range(first, last)])


def after(value, *others):
    return lax.optimization_barrier((value, *others))[0]


def dot(left, right):
    return jnp.dot(left, right, preferred_element_type=jnp.float32)


def turn_kernel(rows, q_heads, used, query_in, grad_in, *refs):
    outs, wide = (refs[: 4 * used], refs[4 * used])
    per = q_heads // used
    for place, source in enumerate((query_in, grad_in)):
        wide[...] = source[...].astype(jnp.float32)
        for head in range(q_heads):
            picked = wide[pl.ds(head, rows, stride=q_heads), :]
            slot, local = divmod(head, per)
            straight, flipped = outs[4 * slot + 2 * place : 4 * slot + 2 * place + 2]
            straight[pl.ds(local * rows, rows), :] = picked.astype(jnp.bfloat16)
            flipped[:, pl.ds(local * rows, rows)] = picked.T.astype(jnp.bfloat16)


def attend_part(count, rows, per, lags, offsets, meta, q_ref, qt_ref, g_ref, gt_ref, *refs):
    pairs = refs[:lags]
    out_ref, qgrad_ref, own_ref = refs[lags : lags + 3]
    terms = refs[lags + 3 : 2 * lags + 2]
    powers, low_tile, tops, sums, out_t, qgrad_t = refs[2 * lags + 2 :]
    shard = meta[0]
    blocks = rows // BLOCK
    head_size = q_ref.shape[1]
    scale = 1.0 / math.sqrt(head_size)
    to_exp2 = scale * LOG2E

    def each_lag(step):
        if count is None:
            step(0)
            for lag in range(1, lags):
                pl.when(shard >= lag)(functools.partial(step, lag))
        else:
            for lag in range(count):
                step(lag)

    def columns(head):
        return slice(head * rows, (head + 1) * rows)

    def fold(op, tile):
        return op(op(tile.reshape(-1, 8, tile.shape[1]), axis=0), axis=0, keepdims=True)

    tops[...] = jnp.full(tops.shape, NEGATIVE, jnp.float32)
    sums[...] = jnp.zeros(sums.shape, jnp.float32)
    out_t[...] = jnp.zeros(out_t.shape, jnp.float32)
    qgrad_t[...] = jnp.zeros(qgrad_t.shape, jnp.float32)

    def score_step(lag):
        query_pos = lax.broadcasted_iota(jnp.int32, (BLOCK, rows), 1)
        key_pos = lax.broadcasted_iota(jnp.int32, (BLOCK, rows), 0)
        query_block = lax.broadcasted_iota(jnp.int32, (1, rows), 1) // BLOCK
        for head in range(per):
            both = dot(pairs[lag][0], qt_ref[:, columns(head)])
            for block in range(blocks):
                tile = both[block * BLOCK : (block + 1) * BLOCK]
                gap = query_pos - key_pos + (lag * rows - block * BLOCK)
                if lag == 0:
                    tile = jnp.where(gap >= 0, tile, NEGATIVE)
                if (lag + 1) * rows > WINDOW:
                    tile = jnp.where(gap < WINDOW, tile, NEGATIVE)
                top = fold(jnp.max, tile)
                power = jnp.exp2((tile - top) * to_exp2)
                powers[lag, block * BLOCK : (block + 1) * BLOCK, columns(head)] = power
                shown = jnp.zeros((1, rows), jnp.int32)
                for seen in range(blocks):
                    distance = lag * blocks + seen - block
                    if 0 <= distance < offsets:
                        shown = jnp.where(query_block == seen, meta[2 + seen * offsets + distance], shown)
                place = lag * blocks + block
                tops[place : place + 1, columns(head)] = jnp.where(shown > 0, top, NEGATIVE)
                sums[place : place + 1, columns(head)] = fold(jnp.sum, power)

    each_lag(score_step)
    top = jnp.max(tops[...], axis=0, keepdims=True)
    factor = jnp.exp2((tops[...] - top) * to_exp2)
    tops[...] = factor / jnp.sum(factor * sums[...], axis=0, keepdims=True)

    def weigh(lag, head):
        tiles = []
        for block in range(blocks):
            place = lag * blocks + block
            power = powers[lag, block * BLOCK : (block + 1) * BLOCK, columns(head)]
            tiles.append(power * tops[place : place + 1, columns(head)])
        return jnp.concatenate(tiles, 0)

    def value_step(lag):
        value_t = pairs[lag][1].T
        for head in range(per):
            low = weigh(lag, head).astype(jnp.bfloat16)
            low_tile[lag, :, columns(head)] = low
            out_t[:, columns(head)] += dot(value_t, low)
        part = dot(low_tile[lag], g_ref[...])
        if lag == 0:
            own_ref[1] = part
        else:
            terms[lag - 1][1] = part.astype(jnp.bfloat16)

    each_lag(value_step)
    attended_t = out_t[...].astype(jnp.bfloat16)
    out_ref[...] = attended_t
    drift = jnp.sum(
        attended_t.astype(jnp.float32) * gt_ref[...].astype(jnp.float32), axis=0, keepdims=True
    )

    def push_step(lag):
        for head in range(per):
            pushed = dot(pairs[lag][1], gt_ref[:, columns(head)])
            low = (weigh(lag, head) * (pushed - drift[:, columns(head)])).astype(jnp.bfloat16)
            low_tile[lag, :, columns(head)] = low

    each_lag(push_step)

    def slope_step(lag):
        key_t = pairs[lag][0].T
        qgrad_t[...] += dot(key_t, low_tile[lag])
        part = dot(low_tile[lag], q_ref[...]) * scale
        if lag == 0:
            own_ref[0] = part
        else:
            terms[lag - 1][0] = part.astype(jnp.bfloat16)

    each_lag(slope_step)
    qgrad_ref[...] = (qgrad_t[...] * scale).astype(jnp.bfloat16)


def attend_kernel(rows, per, lags, offsets, meta, *refs):
    if lags > 4:
        attend_part(None, rows, per, lags, offsets, meta, *refs)
        return
    there = jnp.minimum(meta[0] + 1, lags)
    for count in range(1, lags + 1):
        part = functools.partial(attend_part, count, rows, per, lags, offsets)
        pl.when(there == count)(functools.partial(part, meta, *refs))


def unturn_kernel(rows, q_heads, used, *refs):
    sources, outs, wide = (refs[: 2 * used], refs[2 * used : 2 * used + 2], refs[-1])
    per = q_heads // used
    for place, target in enumerate(outs):
        for head in range(q_heads):
            slot, local = divmod(head, per)
            tile = sources[2 * slot + place][:, pl.ds(local * rows, rows)]
            wide[pl.ds(head, rows, stride=q_heads), :] = tile.astype(jnp.float32).T
        target[...] = wide[...].astype(jnp.bfloat16)


def join_kernel(rows, kv_heads, used, meta, *refs):
    own, other = (refs[:used], refs[used : 2 * used])
    outs, wide = (refs[2 * used : 2 * used + 2], refs[-1])
    first = meta[1]
    for place, target in enumerate(outs):
        for head in range(used):
            mine = own[head][place].astype(jnp.float32)
            theirs = other[head][place].astype(jnp.float32)
            if used == kv_heads:
                wide[pl.ds(head, rows, stride=kv_heads), :] = mine + theirs
            else:
                away = kv_heads - used - first
                wide[pl.ds(first + head, rows, stride=kv_heads), :] = mine
                wide[pl.ds(away + head, rows, stride=kv_heads), :] = theirs
        target[...] = wide[...].astype(jnp.bfloat16)


def body(query, key_states, value_states, grad_out, block_mask):
    rows, q_heads, head_size = query.shape
    kv_heads = key_states.shape[1]
    lags = min(WINDOW // rows, lax.axis_size("seq") - 1) + 1
    used = max(1, q_heads * KV_HEADS // HEADS)
    per = q_heads // used
    width = per * rows
    low, wide = (jnp.bfloat16, jnp.float32)
    core_first = lax.axis_index("sub") * q_heads * KV_HEADS // HEADS
    shard = lax.axis_index("seq")
    meta = jnp.stack([shard, core_first]).astype(jnp.int32)

    def call(kernel, ins, outs, scratch, flops=0, moved=2**20, limit=28):
        return pl.pallas_call(
            kernel,
            in_specs=ins,
            out_specs=[VMEM] * len(outs),
            out_shape=[jax.ShapeDtypeStruct(*o) for o in outs],
            scratch_shapes=[pltpu.VMEM(*s) if isinstance(s, tuple) else s for s in scratch],
            compiler_params=pltpu.CompilerParams(vmem_limit_bytes=limit * 2**20),
            cost_estimate=pl.CostEstimate(flops=flops, bytes_accessed=moved, transcendentals=0),
        )

    packed = []
    for head in range(used - 1, -1, -1):
        states = [after(states, *packed[:1]) for states in (key_states, value_states)]
        picked = [lax.dynamic_index_in_dim(heads, core_first + head, 1, keepdims=False) for heads in states]
        packed.insert(0, jnp.stack(picked, 0))
    turned = call(
        functools.partial(turn_kernel, rows, q_heads, used),
        [VMEM, VMEM],
        [((width, head_size), low), ((head_size, width), low)] * (2 * used),
        [((rows * q_heads, head_size), wide)],
    )(query.reshape(-1, head_size), grad_out.reshape(-1, head_size))
    full_meta = jnp.concatenate([meta, after(block_mask, *packed).reshape(-1)])

    results, sums = ([], [])
    for head in range(used):
        pairs = [packed[head]] + [shifted(packed[head], "seq", lag) for lag in range(1, lags)]
        attended, qgrad, own, *terms = call(
            functools.partial(attend_kernel, rows, per, lags, block_mask.shape[1]),
            [SMEM] + [VMEM] * (4 + lags),
            [((head_size, width), low)] * 2
            + [((2, rows, head_size), wide)]
            + [((2, rows, head_size), low)] * (lags - 1),
            [
                ((lags, rows, width), wide),
                ((lags, rows, width), low),
                ((lags * (rows // BLOCK), width), wide),
                ((lags * (rows // BLOCK), width), wide),
                ((head_size, width), wide),
                ((head_size, width), wide),
            ],
            flops=12 * lags * rows * width * head_size,
        )(full_meta, *turned[4 * head : 4 * head + 4], *pairs)
        results += [attended, qgrad]
        for lag in range(lags - 1, 0, -1):
            own = own + shifted(terms[lag - 1], "seq", -lag).astype(wide)
        sums.append(own.astype(low))

    attended, qgrad = call(
        functools.partial(unturn_kernel, rows, q_heads, used),
        [VMEM] * (2 * used),
        [((rows * q_heads, head_size), low)] * 2,
        [((rows * q_heads, head_size), wide)],
    )(*results)
    others = [lax.ppermute(value, "sub", [(0, 1), (1, 0)]) for value in sums]
    key_grad, value_grad = call(
        functools.partial(join_kernel, rows, kv_heads, used),
        [SMEM] + [VMEM] * (2 * used),
        [((rows * kv_heads, head_size), low)] * 2,
        [((rows * kv_heads, head_size), wide)],
    )(meta, *sums, *others)
    return (
        attended.reshape(rows, q_heads, head_size),
        qgrad.reshape(rows, q_heads, head_size),
        key_grad.reshape(rows, kv_heads, head_size),
        value_grad.reshape(rows, kv_heads, head_size),
    )


def solution(mesh):
    q_spec = P(("groups", "seq"), ("tensor", "sub"), None)
    kv_spec = P(("groups", "seq"), "tensor", None)
    return jax.shard_map(
        body,
        mesh=mesh,
        in_specs=(q_spec, kv_spec, kv_spec, q_spec, P(("groups", "seq"), None)),
        out_specs=(q_spec, q_spec, kv_spec, kv_spec),
        check_vma=False,
    )
```
